32 devices in a mesh: groups: 2 (over x), inputs: 16 (over z, y, core).
Axes of the slice: x: 2, y: 2, z: 4, core: 2. Of those that a mesh axis runs over, the one named last changes fastest.
Arguments:
- samples: bfloat16 [128, 548864], P(('groups', 'inputs')), parts along dimension 0, may hold values from -6 to 6
- filter_coefs: float32 [4, 8192], replicated, may hold values from -0.09375 to 0.09375
Outputs:
- visibilities: bfloat16 [4096, 64, 64], P(('groups', 'inputs')), parts along dimension 0
The draws below stay inside these ranges and needn't reach their ends.
There are 2 independent parts, one for each index of `groups`. The reference program is written for one: setup_inputs(seed, part) draws one part's arguments, and reference() takes and returns one part's arrays. A program takes and returns all parts, laid end to end along the dimension named above; an argument that names none is the same for every part. Nothing has to cross between parts.
All inputs are finite; a program needn't handle non-finite values.
Results may differ from the reference program's by a relative error of at most 0.0085.
Values may be sent and summed in bfloat16 or wider, within the bound.
A program may use at most 128 MiB of HBM per device.

```python
import math
import jax
import jax.numpy as jnp
from jax import lax

NFFT = 8192
TAPS = 4
NSPEC = 64
NCH = 2048
NIN = 64
SAMPLES = 548864


def levels(stream_key, extent, shards, least, top_value):
    factor_of = 1.0
    for axis_at, parts in shards:
        heights = jax.random.uniform(jax.random.fold_in(jax.random.fold_in(stream_key, 6), axis_at), (parts,), jnp.float32, least / len(shards), top_value / len(shards))
        factor_of = factor_of * jnp.repeat(jnp.exp(heights), extent[axis_at] // parts).reshape((-1,) + (1,) * (len(extent) - 1 - axis_at))
    return factor_of


def noise(key, shape, scale, most, cuts=(), held_as=jnp.bfloat16):
    values = scale * jax.random.normal(key, shape, jnp.float32)
    if cuts:
        values = values * levels(key, shape, cuts, -0.22, 0.18)
    return jnp.clip(values, -most, most).astype(held_as)


def setup_inputs(seed: int = 0, part: int = 0) -> dict:
    seeds = jax.random.split(jax.random.key(seed), 3)
    own_keys = jax.random.split(jax.random.fold_in(seeds[2], part), 3)
    samples = noise(own_keys[0], (NIN, SAMPLES), 1.0, 6.0, ((0, 16),))
    filter_coefs = noise(seeds[1], (TAPS, NFFT), (TAPS * NFFT // 8) ** -0.5, 0.09375, (), jnp.float32)
    return dict(samples=samples, filter_coefs=filter_coefs)


HIGH = lax.Precision.HIGHEST


def phase_table(first, second, period):
    rows = lax.broadcasted_iota(jnp.int32, (first, second), 0)
    cols = lax.broadcasted_iota(jnp.int32, (first, second), 1)
    angle = (2.0 * math.pi / period) * ((rows * cols) % period).astype(jnp.float32)
    return jnp.cos(angle), -jnp.sin(angle)


def as_rounded(values):
    return lax.optimization_barrier(values.astype(jnp.bfloat16)).astype(jnp.float32)


def channelise(series, filter_coefs):
    width_b = 128
    width_a = NFFT // width_b
    kept_width = width_b // 4
    frames = series.astype(jnp.float32).reshape(NSPEC + TAPS - 1, NFFT)
    filtered = filter_coefs[0] * frames[0:NSPEC]
    for tap_index in range(1, TAPS):
        filtered = filtered + filter_coefs[tap_index] * frames[tap_index:tap_index + NSPEC]
    grid_view = as_rounded(filtered).reshape(NSPEC, width_a, width_b)
    first_cos, first_sin = phase_table(width_a, width_a, width_a)
    first_cos = as_rounded(first_cos)
    first_sin = as_rounded(first_sin)
    real_one = jnp.einsum("tab,ak->tkb", grid_view, first_cos, precision=HIGH)
    imag_one = jnp.einsum("tab,ak->tkb", grid_view, first_sin, precision=HIGH)
    twist_cos, twist_sin = phase_table(width_a, width_b, NFFT)
    real_two = as_rounded(real_one * twist_cos - imag_one * twist_sin)
    imag_two = as_rounded(real_one * twist_sin + imag_one * twist_cos)
    second_cos, second_sin = phase_table(width_b, width_b, width_b)
    second_cos = as_rounded(second_cos[:, :kept_width])
    second_sin = as_rounded(second_sin[:, :kept_width])
    real_out = (jnp.einsum("tkn,nq->tqk", real_two, second_cos, precision=HIGH)
                - jnp.einsum("tkn,nq->tqk", imag_two, second_sin, precision=HIGH))
    imag_out = (jnp.einsum("tkn,nq->tqk", real_two, second_sin, precision=HIGH)
                + jnp.einsum("tkn,nq->tqk", imag_two, second_cos, precision=HIGH))
    real_part = real_out.reshape(NSPEC, NCH).astype(jnp.bfloat16)
    imag_part = imag_out.reshape(NSPEC, NCH).astype(jnp.bfloat16)
    return jnp.concatenate([real_part.T, imag_part.T], axis=1)


def correlate_block(block):
    values = block.astype(jnp.float32)
    rotated = jnp.concatenate([-values[..., NSPEC:], values[..., :NSPEC]], axis=-1)
    real_sum = jnp.einsum("ikt,jkt->kij", values, values, precision=HIGH)
    imag_sum = jnp.einsum("ikt,jkt->kij", values, rotated, precision=HIGH)
    rows = lax.broadcasted_iota(jnp.int32, (NIN, NIN), 0)
    cols = lax.broadcasted_iota(jnp.int32, (NIN, NIN), 1)
    return (jnp.where(rows >= cols, real_sum, imag_sum) / NSPEC).astype(jnp.bfloat16)


def reference(samples, filter_coefs):
    spectra = lax.map(lambda series: channelise(series, filter_coefs), samples)
    block_size = 32
    blocks = spectra.reshape(NIN, NCH // block_size, block_size, 2 * NSPEC).transpose(1, 0, 2, 3)
    result = lax.map(correlate_block, blocks)
    return result.reshape(NCH, NIN, NIN)
```

```python
import functools
import math

import jax
import jax.numpy as jnp
import numpy as np
from jax import lax
from jax.experimental import pallas as pl
from jax.experimental.pallas import tpu as pltpu
from jax.sharding import PartitionSpec as P


def phase_table(first, second, period):
    rows = lax.broadcasted_iota(jnp.int32, (first, second), 0)
    cols = lax.broadcasted_iota(jnp.int32, (first, second), 1)
    angle = 2.0 * math.pi / period * (rows * cols % period).astype(jnp.float32)
    return (jnp.cos(angle), -jnp.sin(angle))


def correlate_items(block):
    count = block.shape[0]
    nspec_local = block.shape[2] // 2
    rotated = jnp.concatenate([-block[..., nspec_local:], block[..., :nspec_local]], axis=-1)
    real_sum = jnp.einsum("ikt,jkt->kij", block, block, preferred_element_type=jnp.float32)
    imag_sum = jnp.einsum("ikt,jkt->kij", block, rotated, preferred_element_type=jnp.float32)
    rows = lax.broadcasted_iota(jnp.int32, (count, count), 0)
    cols = lax.broadcasted_iota(jnp.int32, (count, count), 1)
    return (jnp.where(rows >= cols, real_sum, imag_sum) / nspec_local).astype(jnp.bfloat16)


def correlate_turned(block):
    flat_block = block.reshape(block.shape[0], block.shape[2], block.shape[3])
    return correlate_items(flat_block)


def plain_body(samples, filter_coefs):
    in_local, total = samples.shape
    taps_count, nfft_local = filter_coefs.shape
    frame_count = total // nfft_local
    nspec_local = frame_count - taps_count + 1
    width_b = 128
    width_a = nfft_local // width_b
    kept_width = width_b // 4
    frames = samples.reshape(in_local, frame_count, nfft_local).astype(jnp.float32)
    filtered = filter_coefs[0] * frames[:, 0:nspec_local]
    for tap_index in range(1, taps_count):
        filtered = (
            filtered + filter_coefs[tap_index] * frames[:, tap_index : tap_index + nspec_local]
        )
    grid_view = filtered.astype(jnp.bfloat16).reshape(in_local, nspec_local, width_a, width_b)
    first_cos, first_sin = phase_table(width_a, width_a, width_a)
    first_table = jnp.concatenate([first_cos, first_sin], axis=1).astype(jnp.bfloat16)
    first_out = jnp.einsum(
        "itab,ak->itkb", grid_view, first_table, preferred_element_type=jnp.float32
    )
    real_one = first_out[:, :, :width_a]
    imag_one = first_out[:, :, width_a:]
    twist_cos, twist_sin = phase_table(width_a, width_b, nfft_local)
    real_two = real_one * twist_cos - imag_one * twist_sin
    imag_two = real_one * twist_sin + imag_one * twist_cos
    stacked = jnp.concatenate(
        [real_two.astype(jnp.bfloat16), imag_two.astype(jnp.bfloat16)], axis=3
    )
    second_cos, second_sin = phase_table(width_b, width_b, width_b)
    second_cos = second_cos[:, :kept_width]
    second_sin = second_sin[:, :kept_width]
    upper_rows = jnp.concatenate([second_cos, second_sin], axis=1)
    lower_rows = jnp.concatenate([-second_sin, second_cos], axis=1)
    second_table = jnp.concatenate([upper_rows, lower_rows], axis=0).astype(jnp.bfloat16)
    second_out = jnp.einsum(
        "itkn,nq->iqkt", stacked, second_table, preferred_element_type=jnp.float32
    )
    real_out = second_out[:, :kept_width]
    imag_out = second_out[:, kept_width:]
    channels = width_a * kept_width
    spectra = jnp.concatenate(
        [real_out.astype(jnp.bfloat16), imag_out.astype(jnp.bfloat16)], axis=3
    )
    spectra = spectra.reshape(in_local, channels, 2 * nspec_local)
    peers = lax.axis_size("inputs")
    per_peer = channels // peers
    owner_view = spectra.reshape(in_local, peers, per_peer, 2 * nspec_local)
    result = correlate_turned(
        lax.all_to_all(owner_view, "inputs", split_axis=1, concat_axis=0, tiled=True)
    )
    return result


WIDTH_B = 128
BF16 = jnp.bfloat16
F32 = jnp.float32
NT = (((1,), (1,)), ((), ()))


def np_phase(first, second, period):
    turns = np.outer(np.arange(first), np.arange(second)) % period
    angle = np.float32(2.0 * math.pi / period) * turns.astype(np.float32)
    return np.cos(angle), -np.sin(angle)


def make_tables(in_local, width_a, kept):
    nfft = width_a * WIDTH_B
    first = np.concatenate([t.T for t in np_phase(width_a, width_a, width_a)], axis=0)
    first = np.kron(first, np.eye(in_local, dtype=np.float32))
    twist = np.concatenate(
        [np.repeat(t, in_local, axis=0) for t in np_phase(width_a, WIDTH_B, nfft)], axis=0
    )
    cos_b, sin_b = (t[:, :kept].T for t in np_phase(WIDTH_B, WIDTH_B, WIDTH_B))
    second = np.concatenate(
        [np.concatenate([cos_b, -sin_b], axis=1), np.concatenate([sin_b, cos_b], axis=1)], axis=0
    )
    return jnp.asarray(first, BF16), jnp.asarray(twist, F32), jnp.asarray(second, BF16)


def spectra_kernel(
    dims, x_ref, coef_ref, first_ref, twist_ref, second_ref, recv_ref,
    real_ref, imag_ref, turn_ref, send_ref, send_sem, recv_sem, own_sem,
):
    peers, in_local, nspec, taps, kept, chunks = dims
    rows = first_ref.shape[1]
    width_a = rows // in_local
    pairs = width_a // 2
    step = pairs // chunks
    me = lax.axis_index("inputs")

    barrier = pltpu.get_barrier_semaphore()

    def greet(o, carry):
        pl.semaphore_signal(
            barrier, inc=1, device_id={"inputs": lax.rem(me + o, peers)},
            device_id_type=pl.DeviceIdType.MESH,
        )
        return carry

    lax.fori_loop(1, peers, greet, 0)

    def one_spectrum(t, carry):
        acc = None
        for m in range(taps):
            frame = x_ref[pl.ds(pl.multiple_of((t + m) * rows, rows), rows), :].astype(F32)
            term = coef_ref[m * rows:(m + 1) * rows, :] * frame
            acc = term if acc is None else acc + term
        out = jnp.dot(first_ref[...], acc.astype(BF16), preferred_element_type=F32)
        re, im = out[:rows], out[rows:]
        w_re, w_im = twist_ref[:rows, :], twist_ref[rows:, :]
        real_ref[pl.ds(t, rows, stride=nspec), :] = re * w_re - im * w_im
        imag_ref[pl.ds(t, rows, stride=nspec), :] = re * w_im + im * w_re
        return carry

    lax.fori_loop(0, nspec, one_spectrum, 0)
    pl.semaphore_wait(barrier, peers - 1)

    span = in_local * nspec
    per_dest = kept // peers * in_local

    def channel_pair(kp, carry):
        parts = []
        for kk in range(2):
            at = pl.ds(pl.multiple_of((kp * 2 + kk) * span, span), span)
            both = jnp.concatenate(
                [real_ref[at, :].astype(BF16), imag_ref[at, :].astype(BF16)], axis=1
            )
            res = lax.dot_general(second_ref[...], both, NT, preferred_element_type=F32)
            for i in range(in_local):
                cols = slice(i * nspec, (i + 1) * nspec)
                turn_ref[pl.ds(kk * kept * in_local + i, kept, stride=in_local), :] = (
                    jnp.concatenate([res[:kept, cols], res[kept:, cols]], axis=1)
                )
            part = turn_ref[kk * kept * in_local:(kk + 1) * kept * in_local, :]
            parts.append(part.reshape(peers, per_dest, 2 * nspec))
        send_ref[:, kp] = jnp.concatenate(parts, axis=1).astype(BF16)
        return carry

    def remote(c, o):
        dest = lax.rem(me + o, peers)
        at = pl.ds(c * step, step)
        return pltpu.make_async_remote_copy(
            src_ref=send_ref.at[dest, at], dst_ref=recv_ref.at[me, at],
            send_sem=send_sem.at[c, o], recv_sem=recv_sem.at[c, o],
            device_id={"inputs": dest}, device_id_type=pl.DeviceIdType.MESH,
        )

    def chunk(c, carry):
        lax.fori_loop(c * step, (c + 1) * step, channel_pair, 0)

        def push(n, carry):
            remote(c, lax.rem(n + peers // 2 - 1, peers - 1) + 1).start()
            return carry

        lax.fori_loop(0, peers - 1, push, 0)
        return carry

    lax.fori_loop(0, chunks, chunk, 0)
    own = pltpu.make_async_copy(send_ref.at[me], recv_ref.at[me], own_sem)
    own.start()

    def finish(n, carry):
        remote(n // (peers - 1), n % (peers - 1) + 1).wait()
        return carry

    lax.fori_loop(0, chunks * (peers - 1), finish, 0)
    own.wait()


def correlate_kernel(dims, x_ref, order_ref, out_ref, vis_ref):
    peers, in_local, nspec, pairs = dims
    count = peers * in_local
    per = x_ref.shape[2] // in_local
    channels = pairs * per
    halves = per // 2
    i_at = lax.broadcasted_iota(jnp.int32, (count, count), 0)
    j_at = lax.broadcasted_iota(jnp.int32, (count, count), 1)

    def one_pair(kp, carry):
        rows = x_ref[:, kp].reshape(peers * per * in_local, 2 * nspec)
        lined = jnp.dot(order_ref[...], rows, preferred_element_type=F32)
        turned = jnp.concatenate([-lined[:, nspec:], lined[:, :nspec]], axis=1).astype(BF16)
        lined = lined.astype(BF16)
        for s in range(per):
            block = lined[s * count:(s + 1) * count]
            rotated = turned[s * count:(s + 1) * count]
            re = lax.dot_general(block, block, NT, preferred_element_type=F32)
            im = lax.dot_general(block, rotated, NT, preferred_element_type=F32)
            c = (s % halves) * 2 * pairs + kp * 2 + s // halves
            vis_ref[pl.ds(c, count, stride=channels), :] = (
                jnp.where(i_at >= j_at, re, im) * (1.0 / nspec)
            )
        return carry

    lax.fori_loop(0, pairs, one_pair, 0)

    def one_row(i, carry):
        block = vis_ref[pl.ds(pl.multiple_of(i * channels, channels), channels), :]
        out_ref[i] = block.T.astype(BF16)
        return carry

    lax.fori_loop(0, count, one_row, 0)


def kernel_body(peers, kept, samples, filter_coefs):
    in_local, total = samples.shape
    taps, nfft = filter_coefs.shape
    width_a = nfft // WIDTH_B
    nspec = total // nfft - taps + 1
    rows = width_a * in_local
    pairs = width_a // 2
    chunks = 4
    per = 2 * (kept // peers)
    count = peers * in_local
    x = samples.reshape(in_local, total // WIDTH_B, WIDTH_B).transpose(1, 0, 2)
    x = x.reshape(total // WIDTH_B * in_local, WIDTH_B)
    coefs = filter_coefs.reshape(taps, width_a, 1, WIDTH_B)
    coefs = jnp.broadcast_to(coefs, (taps, width_a, in_local, WIDTH_B))
    coefs = coefs.reshape(taps * rows, WIDTH_B)
    first, twist, second = make_tables(in_local, width_a, kept)
    vmem = pl.BlockSpec(memory_space=pltpu.VMEM)
    turned = pl.pallas_call(
        functools.partial(spectra_kernel, (peers, in_local, nspec, taps, kept, chunks)),
        out_shape=jax.ShapeDtypeStruct((peers, pairs, per * in_local, 2 * nspec), BF16),
        in_specs=[vmem] * 5,
        out_specs=pl.BlockSpec(memory_space=pl.ANY),
        scratch_shapes=[
            pltpu.VMEM((rows * nspec, WIDTH_B), F32),
            pltpu.VMEM((rows * nspec, WIDTH_B), F32),
            pltpu.VMEM((2 * kept * in_local, 2 * nspec), F32),
            pltpu.VMEM((peers, pairs, per * in_local, 2 * nspec), BF16),
            pltpu.SemaphoreType.DMA((chunks, peers)),
            pltpu.SemaphoreType.DMA((chunks, peers)),
            pltpu.SemaphoreType.DMA,
        ],
        compiler_params=pltpu.CompilerParams(
            collective_id=0, has_side_effects=True, vmem_limit_bytes=48 * 2**20
        ),
        name="spectra",
    )(x, coefs, first, twist, second)
    order = np.zeros((per, peers, in_local, peers, per, in_local), np.float32)
    for s in range(per):
        for p in range(peers):
            order[s, p, range(in_local), p, s, range(in_local)] = 1
    order = jnp.asarray(order.reshape(per * count, per * count), BF16)
    channels = pairs * per
    out = pl.pallas_call(
        functools.partial(correlate_kernel, (peers, in_local, nspec, pairs)),
        out_shape=jax.ShapeDtypeStruct((count, count, channels), BF16),
        in_specs=[vmem] * 2,
        out_specs=vmem,
        scratch_shapes=[pltpu.VMEM((count * channels, count), F32)],
        compiler_params=pltpu.CompilerParams(vmem_limit_bytes=32 * 2**20),
        name="correlate",
    )(turned, order)
    return out.transpose(2, 0, 1)


def solution(mesh):
    peers = mesh.shape["inputs"]

    def body(samples, filter_coefs):
        in_local = samples.shape[0]
        kept = WIDTH_B // 4
        whole_q = kept % peers == 0
        if whole_q and (2 * in_local * (kept // peers)) % 16 == 0:
            return kernel_body(peers, kept, samples, filter_coefs)
        return plain_body(samples, filter_coefs)

    return jax.shard_map(
        body,
        mesh=mesh,
        in_specs=(P(("groups", "inputs"), None), P()),
        out_specs=P(("groups", "inputs"), None, None),
        check_vma=False,
    )
```

```python
import functools
import math

import jax
import jax.numpy as jnp
import numpy as np
from jax import lax
from jax.experimental import pallas as pl
from jax.experimental.pallas import tpu as pltpu
from jax.sharding import PartitionSpec as P


def phase_table(first, second, period):
    rows = lax.broadcasted_iota(jnp.int32, (first, second), 0)
    cols = lax.broadcasted_iota(jnp.int32, (first, second), 1)
    angle = 2.0 * math.pi / period * (rows * cols % period).astype(jnp.float32)
    return (jnp.cos(angle), -jnp.sin(angle))


def correlate_items(block):
    count = block.shape[0]
    nspec_local = block.shape[2] // 2
    rotated = jnp.concatenate([-block[..., nspec_local:], block[..., :nspec_local]], axis=-1)
    real_sum = jnp.einsum("ikt,jkt->kij", block, block, preferred_element_type=jnp.float32)
    imag_sum = jnp.einsum("ikt,jkt->kij", block, rotated, preferred_element_type=jnp.float32)
    rows = lax.broadcasted_iota(jnp.int32, (count, count), 0)
    cols = lax.broadcasted_iota(jnp.int32, (count, count), 1)
    return (jnp.where(rows >= cols, real_sum, imag_sum) / nspec_local).astype(jnp.bfloat16)


def correlate_turned(block):
    flat_block = block.reshape(block.shape[0], block.shape[2], block.shape[3])
    return correlate_items(flat_block)


def plain_body(samples, filter_coefs):
    in_local, total = samples.shape
    taps_count, nfft_local = filter_coefs.shape
    frame_count = total // nfft_local
    nspec_local = frame_count - taps_count + 1
    width_b = 128
    width_a = nfft_local // width_b
    kept_width = width_b // 4
    frames = samples.reshape(in_local, frame_count, nfft_local).astype(jnp.float32)
    filtered = filter_coefs[0] * frames[:, 0:nspec_local]
    for tap_index in range(1, taps_count):
        filtered = (
            filtered + filter_coefs[tap_index] * frames[:, tap_index : tap_index + nspec_local]
        )
    grid_view = filtered.astype(jnp.bfloat16).reshape(in_local, nspec_local, width_a, width_b)
    first_cos, first_sin = phase_table(width_a, width_a, width_a)
    first_table = jnp.concatenate([first_cos, first_sin], axis=1).astype(jnp.bfloat16)
    first_out = jnp.einsum(
        "itab,ak->itkb", grid_view, first_table, preferred_element_type=jnp.float32
    )
    real_one = first_out[:, :, :width_a]
    imag_one = first_out[:, :, width_a:]
    twist_cos, twist_sin = phase_table(width_a, width_b, nfft_local)
    real_two = real_one * twist_cos - imag_one * twist_sin
    imag_two = real_one * twist_sin + imag_one * twist_cos
    stacked = jnp.concatenate(
        [real_two.astype(jnp.bfloat16), imag_two.astype(jnp.bfloat16)], axis=3
    )
    second_cos, second_sin = phase_table(width_b, width_b, width_b)
    second_cos = second_cos[:, :kept_width]
    second_sin = second_sin[:, :kept_width]
    upper_rows = jnp.concatenate([second_cos, second_sin], axis=1)
    lower_rows = jnp.concatenate([-second_sin, second_cos], axis=1)
    second_table = jnp.concatenate([upper_rows, lower_rows], axis=0).astype(jnp.bfloat16)
    second_out = jnp.einsum(
        "itkn,nq->iqkt", stacked, second_table, preferred_element_type=jnp.float32
    )
    real_out = second_out[:, :kept_width]
    imag_out = second_out[:, kept_width:]
    channels = width_a * kept_width
    spectra = jnp.concatenate(
        [real_out.astype(jnp.bfloat16), imag_out.astype(jnp.bfloat16)], axis=3
    )
    spectra = spectra.reshape(in_local, channels, 2 * nspec_local)
    peers = lax.axis_size("inputs")
    per_peer = channels // peers
    owner_view = spectra.reshape(in_local, peers, per_peer, 2 * nspec_local)
    result = correlate_turned(
        lax.all_to_all(owner_view, "inputs", split_axis=1, concat_axis=0, tiled=True)
    )
    return result


WIDTH_B = 128
BF16 = jnp.bfloat16
F32 = jnp.float32
NT = (((1,), (1,)), ((), ()))


def np_phase(first, second, period):
    turns = np.outer(np.arange(first), np.arange(second)) % period
    angle = np.float32(2.0 * math.pi / period) * turns.astype(np.float32)
    return np.cos(angle), -np.sin(angle)


def make_tables(in_local, width_a, kept):
    nfft = width_a * WIDTH_B
    first = np.concatenate([t.T for t in np_phase(width_a, width_a, width_a)], axis=0)
    first = np.kron(first, np.eye(in_local, dtype=np.float32))
    twist = np.concatenate(
        [np.repeat(t, in_local, axis=0) for t in np_phase(width_a, WIDTH_B, nfft)], axis=0
    )
    cos_b, sin_b = (t[:, :kept].T for t in np_phase(WIDTH_B, WIDTH_B, WIDTH_B))
    second = np.concatenate(
        [np.concatenate([cos_b, -sin_b], axis=1), np.concatenate([sin_b, cos_b], axis=1)], axis=0
    )
    return jnp.asarray(first, BF16), jnp.asarray(twist, F32), jnp.asarray(second, BF16)


def correlator_kernel(
    dims, x_any, coef_any, first_any, twist_any, second_any, order_any, vis_ref,
    x_ref, coef_in, first_ref, twist_ref, second_ref, order_ref, coef_ref,
    real_ref, imag_ref, turn_ref, send_ref, recv_ref,
    load_sem, x_sem, send_sem, recv_sem, own_sem,
):
    peers, in_local, nspec, taps, kept, chunks, loads, pad = dims
    rows = first_ref.shape[1]
    width_a = rows // in_local
    pairs = width_a // 2
    step = pairs // chunks
    slot = nspec + pad
    me = lax.axis_index("inputs")

    barrier = pltpu.get_barrier_semaphore()

    def greet(o, carry):
        pl.semaphore_signal(
            barrier, inc=1, device_id={"inputs": lax.rem(me + o, peers)},
            device_id_type=pl.DeviceIdType.MESH,
        )
        return carry

    lax.fori_loop(1, peers, greet, 0)

    t_load = nspec // loads

    def load_frames(n):
        start = 0 if n == 0 else n * t_load + taps - 1
        at = pl.ds(start * rows, ((n + 1) * t_load + taps - 1 - start) * rows)
        return pltpu.make_async_copy(x_any.at[at], x_ref.at[at], x_sem.at[n])

    small = [
        pltpu.make_async_copy(src, dst, load_sem.at[n])
        for n, (src, dst) in enumerate((
            (coef_any, coef_in), (first_any, first_ref), (twist_any, twist_ref),
            (second_any, second_ref), (order_any, order_ref),
        ))
    ]
    small[0].start()
    load_frames(0).start()
    for copy in small[1:]:
        copy.start()
    for n in range(1, loads):
        load_frames(n).start()

    small[0].wait()
    for m in range(taps):
        tap = coef_in[pl.ds(m, width_a, stride=taps), :]
        for i in range(in_local):
            coef_ref[pl.ds(m * rows + i, width_a, stride=in_local), :] = tap
    for copy in small[1:]:
        copy.wait()

    def one_spectrum(t, carry):
        acc = None
        for m in range(taps):
            frame = x_ref[pl.ds(pl.multiple_of((t + m) * rows, rows), rows), :].astype(F32)
            term = coef_ref[m * rows:(m + 1) * rows, :] * frame
            acc = term if acc is None else acc + term
        out = jnp.dot(first_ref[...], acc.astype(BF16), preferred_element_type=F32)
        re, im = out[:rows], out[rows:]
        w_re, w_im = twist_ref[:rows, :], twist_ref[rows:, :]
        real_ref[pl.ds(t, rows, stride=slot), :] = re * w_re - im * w_im
        imag_ref[pl.ds(t, rows, stride=slot), :] = re * w_im + im * w_re
        return carry

    for n in range(loads):
        load_frames(n).wait()
        lax.fori_loop(n * t_load, (n + 1) * t_load, one_spectrum, 0, unroll=2)
    pl.semaphore_wait(barrier, peers - 1)

    per_dest = kept // peers * in_local

    def channel_pair(kp, carry):
        parts = []
        for kk in range(2):
            both = []
            for i in range(in_local):
                at = pl.ds(((kp * 2 + kk) * in_local + i) * slot, nspec)
                both.append(jnp.concatenate(
                    [real_ref[at, :].astype(BF16), imag_ref[at, :].astype(BF16)], axis=1
                ))
            both = jnp.concatenate(both, axis=0)
            res = lax.dot_general(second_ref[...], both, NT, preferred_element_type=F32)
            for i in range(in_local):
                cols = slice(i * nspec, (i + 1) * nspec)
                turn_ref[pl.ds(kk * kept * in_local + i, kept, stride=in_local), :] = (
                    jnp.concatenate([res[:kept, cols], res[kept:, cols]], axis=1)
                )
            part = turn_ref[kk * kept * in_local:(kk + 1) * kept * in_local, :]
            parts.append(part.reshape(peers, per_dest, 2 * nspec))
        send_ref[:, kp] = jnp.concatenate(parts, axis=1).astype(BF16)
        return carry

    def remote(c, o):
        dest = lax.rem(me + o, peers)
        at = pl.ds(c * step, step)
        return pltpu.make_async_remote_copy(
            src_ref=send_ref.at[dest, at], dst_ref=recv_ref.at[me, at],
            send_sem=send_sem.at[c, o], recv_sem=recv_sem.at[c, o],
            device_id={"inputs": dest}, device_id_type=pl.DeviceIdType.MESH,
        )

    def chunk(c, carry):
        lax.fori_loop(0, step, lambda n, u: channel_pair(c * step + n, u), 0, unroll=2)

        def push(n, carry):
            remote(c, lax.rem(n + peers // 2 - 1, peers - 1) + 1).start()
            return carry

        lax.fori_loop(0, peers - 1, push, 0)
        return carry

    lax.fori_loop(0, chunks, chunk, 0)
    own = pltpu.make_async_copy(send_ref.at[me], recv_ref.at[me], own_sem)
    own.start()
    own.wait()

    count = peers * in_local
    per = 2 * (kept // peers)
    halves = per // 2
    channels = pairs * per
    i_at = lax.broadcasted_iota(jnp.int32, (count, count), 0)
    j_at = lax.broadcasted_iota(jnp.int32, (count, count), 1)

    def correlate_pair(kp, carry):
        block_rows = recv_ref[:, kp].reshape(per * count, 2 * nspec)
        lined = jnp.dot(order_ref[...], block_rows, preferred_element_type=F32)
        turned = jnp.concatenate([-lined[:, nspec:], lined[:, :nspec]], axis=1).astype(BF16)
        lined = lined.astype(BF16)
        for s in range(per):
            block = lined[s * count:(s + 1) * count]
            rotated = turned[s * count:(s + 1) * count]
            re = lax.dot_general(block, block, NT, preferred_element_type=F32)
            im = lax.dot_general(block, rotated, NT, preferred_element_type=F32)
            vis = jnp.where(i_at >= j_at, re, im) * (1.0 / nspec)
            c = (s % halves) * 2 * pairs + kp * 2 + s // halves
            vis_ref[pl.ds(c, count // 2, stride=channels), :] = jnp.concatenate(
                [vis[:count // 2], vis[count // 2:]], axis=1
            )
        return carry

    def receive(c, carry):
        def arrive(o, carry):
            remote(c, o).wait_recv()
            return carry

        lax.fori_loop(1, peers, arrive, 0)
        lax.fori_loop(0, step, lambda n, u: correlate_pair(c * step + n, u), 0, unroll=2)
        return carry

    lax.fori_loop(0, chunks, receive, 0)

    def finish(n, carry):
        remote(n // (peers - 1), n % (peers - 1) + 1).wait_send()
        return carry

    lax.fori_loop(0, chunks * (peers - 1), finish, 0)


def turn_kernel(channels, vis_ref, out_ref):
    half = out_ref.shape[0] // 2
    width = out_ref.shape[1]

    def one_row(i, carry):
        block = vis_ref[pl.ds(pl.multiple_of(i * channels, channels), channels), :]
        block = block.T.astype(BF16)
        out_ref[i] = block[:width]
        out_ref[i + half] = block[width:]
        return carry

    lax.fori_loop(0, half, one_row, 0, unroll=4)


def kernel_body(peers, kept, samples, filter_coefs):
    in_local, total = samples.shape
    taps, nfft = filter_coefs.shape
    width_a = nfft // WIDTH_B
    nspec = total // nfft - taps + 1
    rows = width_a * in_local
    pairs = width_a // 2
    chunks = 8
    loads = 4
    pad = 0
    per = 2 * (kept // peers)
    count = peers * in_local
    channels = pairs * per
    x = samples.reshape(in_local, total // WIDTH_B, WIDTH_B).transpose(1, 0, 2)
    x = x.reshape(total // WIDTH_B * in_local, WIDTH_B)
    coefs = filter_coefs.reshape(taps, width_a, WIDTH_B).transpose(1, 0, 2)
    coefs = coefs.reshape(width_a * taps, WIDTH_B)
    first, twist, second = make_tables(in_local, width_a, kept)
    order = np.zeros((per, peers, in_local, peers, per, in_local), np.float32)
    for s in range(per):
        for p in range(peers):
            order[s, p, range(in_local), p, s, range(in_local)] = 1
    order = jnp.asarray(order.reshape(per * count, per * count), BF16)
    blocks = (peers, pairs, per * in_local, 2 * nspec)
    inputs = (x, coefs, first, twist, second, order)
    vis = pl.pallas_call(
        functools.partial(
            correlator_kernel, (peers, in_local, nspec, taps, kept, chunks, loads, pad)
        ),
        out_shape=jax.ShapeDtypeStruct((count // 2 * channels, 2 * count), F32),
        in_specs=[pl.BlockSpec(memory_space=pl.ANY)] * len(inputs),
        out_specs=pl.BlockSpec(memory_space=pltpu.VMEM),
        scratch_shapes=[pltpu.VMEM(a.shape, a.dtype) for a in inputs] + [
            pltpu.VMEM((taps * rows, WIDTH_B), F32),
            pltpu.VMEM((rows * (nspec + pad), WIDTH_B), F32),
            pltpu.VMEM((rows * (nspec + pad), WIDTH_B), F32),
            pltpu.VMEM((2 * kept * in_local, 2 * nspec), F32),
            pltpu.VMEM(blocks, BF16),
            pltpu.VMEM(blocks, BF16),
            pltpu.SemaphoreType.DMA((len(inputs) - 1,)),
            pltpu.SemaphoreType.DMA((loads,)),
            pltpu.SemaphoreType.DMA((chunks, peers)),
            pltpu.SemaphoreType.DMA((chunks, peers)),
            pltpu.SemaphoreType.DMA,
        ],
        compiler_params=pltpu.CompilerParams(
            collective_id=0, has_side_effects=True, vmem_limit_bytes=56 * 2**20
        ),
        name="correlator",
    )(*inputs)
    out = pl.pallas_call(
        functools.partial(turn_kernel, channels),
        out_shape=jax.ShapeDtypeStruct((count, count, channels), BF16),
        in_specs=[pl.BlockSpec(memory_space=pltpu.VMEM)],
        out_specs=pl.BlockSpec(memory_space=pltpu.VMEM),
        compiler_params=pltpu.CompilerParams(vmem_limit_bytes=32 * 2**20),
        name="turn",
    )(vis)
    return out.transpose(2, 0, 1)


def solution(mesh):
    peers = mesh.shape["inputs"]

    def body(samples, filter_coefs):
        in_local = samples.shape[0]
        kept = WIDTH_B // 4
        whole_q = kept % peers == 0
        if whole_q and (2 * in_local * (kept // peers)) % 16 == 0:
            return kernel_body(peers, kept, samples, filter_coefs)
        return plain_body(samples, filter_coefs)

    return jax.shard_map(
        body,
        mesh=mesh,
        in_specs=(P(("groups", "inputs"), None), P()),
        out_specs=P(("groups", "inputs"), None, None),
        check_vma=False,
    )
```

```python
import functools
import math

import jax
import jax.numpy as jnp
import numpy as np
from jax import lax
from jax.experimental import pallas as pl
from jax.experimental.pallas import tpu as pltpu
from jax.sharding import PartitionSpec as P


def phase_table(first, second, period):
    rows = lax.broadcasted_iota(jnp.int32, (first, second), 0)
    cols = lax.broadcasted_iota(jnp.int32, (first, second), 1)
    angle = 2.0 * math.pi / period * (rows * cols % period).astype(jnp.float32)
    return (jnp.cos(angle), -jnp.sin(angle))


def correlate_items(block):
    count = block.shape[0]
    nspec_local = block.shape[2] // 2
    rotated = jnp.concatenate([-block[..., nspec_local:], block[..., :nspec_local]], axis=-1)
    real_sum = jnp.einsum("ikt,jkt->kij", block, block, preferred_element_type=jnp.float32)
    imag_sum = jnp.einsum("ikt,jkt->kij", block, rotated, preferred_element_type=jnp.float32)
    rows = lax.broadcasted_iota(jnp.int32, (count, count), 0)
    cols = lax.broadcasted_iota(jnp.int32, (count, count), 1)
    return (jnp.where(rows >= cols, real_sum, imag_sum) / nspec_local).astype(jnp.bfloat16)


def correlate_turned(block):
    flat_block = block.reshape(block.shape[0], block.shape[2], block.shape[3])
    return correlate_items(flat_block)


def plain_body(samples, filter_coefs):
    in_local, total = samples.shape
    taps_count, nfft_local = filter_coefs.shape
    frame_count = total // nfft_local
    nspec_local = frame_count - taps_count + 1
    width_b = 128
    width_a = nfft_local // width_b
    kept_width = width_b // 4
    frames = samples.reshape(in_local, frame_count, nfft_local).astype(jnp.float32)
    filtered = filter_coefs[0] * frames[:, 0:nspec_local]
    for tap_index in range(1, taps_count):
        filtered = (
            filtered + filter_coefs[tap_index] * frames[:, tap_index : tap_index + nspec_local]
        )
    grid_view = filtered.astype(jnp.bfloat16).reshape(in_local, nspec_local, width_a, width_b)
    first_cos, first_sin = phase_table(width_a, width_a, width_a)
    first_table = jnp.concatenate([first_cos, first_sin], axis=1).astype(jnp.bfloat16)
    first_out = jnp.einsum(
        "itab,ak->itkb", grid_view, first_table, preferred_element_type=jnp.float32
    )
    real_one = first_out[:, :, :width_a]
    imag_one = first_out[:, :, width_a:]
    twist_cos, twist_sin = phase_table(width_a, width_b, nfft_local)
    real_two = real_one * twist_cos - imag_one * twist_sin
    imag_two = real_one * twist_sin + imag_one * twist_cos
    stacked = jnp.concatenate(
        [real_two.astype(jnp.bfloat16), imag_two.astype(jnp.bfloat16)], axis=3
    )
    second_cos, second_sin = phase_table(width_b, width_b, width_b)
    second_cos = second_cos[:, :kept_width]
    second_sin = second_sin[:, :kept_width]
    upper_rows = jnp.concatenate([second_cos, second_sin], axis=1)
    lower_rows = jnp.concatenate([-second_sin, second_cos], axis=1)
    second_table = jnp.concatenate([upper_rows, lower_rows], axis=0).astype(jnp.bfloat16)
    second_out = jnp.einsum(
        "itkn,nq->iqkt", stacked, second_table, preferred_element_type=jnp.float32
    )
    real_out = second_out[:, :kept_width]
    imag_out = second_out[:, kept_width:]
    channels = width_a * kept_width
    spectra = jnp.concatenate(
        [real_out.astype(jnp.bfloat16), imag_out.astype(jnp.bfloat16)], axis=3
    )
    spectra = spectra.reshape(in_local, channels, 2 * nspec_local)
    peers = lax.axis_size("inputs")
    per_peer = channels // peers
    owner_view = spectra.reshape(in_local, peers, per_peer, 2 * nspec_local)
    result = correlate_turned(
        lax.all_to_all(owner_view, "inputs", split_axis=1, concat_axis=0, tiled=True)
    )
    return result


WIDTH_B = 128
BF16 = jnp.bfloat16
F32 = jnp.float32
NT = (((1,), (1,)), ((), ()))


def np_phase(first, second, period):
    turns = np.outer(np.arange(first), np.arange(second)) % period
    angle = np.float32(2.0 * math.pi / period) * turns.astype(np.float32)
    return np.cos(angle), -np.sin(angle)


def make_tables(in_local, width_a, kept):
    nfft = width_a * WIDTH_B
    first = np.concatenate([t.T for t in np_phase(width_a, width_a, width_a)], axis=0)
    first = np.kron(first, np.eye(in_local, dtype=np.float32))
    twist = np.concatenate(
        [np.repeat(t, in_local, axis=0) for t in np_phase(width_a, WIDTH_B, nfft)], axis=0
    )
    cos_b, sin_b = (t[:, :kept].T for t in np_phase(WIDTH_B, WIDTH_B, WIDTH_B))
    second = np.concatenate(
        [np.concatenate([cos_b, -sin_b], axis=1), np.concatenate([sin_b, cos_b], axis=1)], axis=0
    )
    return jnp.asarray(first, BF16), jnp.asarray(twist, F32), jnp.asarray(second, BF16)


def correlator_kernel(
    dims, x_any, coef_any, first_any, twist_any, second_any, order_any, vis_ref,
    x_ref, coef_in, first_ref, twist_ref, second_ref, order_ref, coef_ref,
    real_ref, imag_ref, turn_ref, send_ref, recv_ref,
    load_sem, x_sem, send_sem, recv_sem, own_sem,
):
    peers, in_local, nspec, taps, kept, chunks, loads, pad = dims
    rows = first_ref.shape[1]
    width_a = rows // in_local
    pairs = width_a // 2
    step = pairs // chunks
    slot = nspec + pad
    me = lax.axis_index("inputs")

    barrier = pltpu.get_barrier_semaphore()

    def greet(o, carry):
        pl.semaphore_signal(
            barrier, inc=1, device_id={"inputs": lax.rem(me + o, peers)},
            device_id_type=pl.DeviceIdType.MESH,
        )
        return carry

    lax.fori_loop(1, peers, greet, 0)

    t_load = nspec // loads

    def load_frames(n):
        start = 0 if n == 0 else n * t_load + taps - 1
        at = pl.ds(start * rows, ((n + 1) * t_load + taps - 1 - start) * rows)
        return pltpu.make_async_copy(x_any.at[at], x_ref.at[at], x_sem.at[n])

    small = [
        pltpu.make_async_copy(src, dst, load_sem.at[n])
        for n, (src, dst) in enumerate((
            (coef_any, coef_in), (first_any, first_ref), (twist_any, twist_ref),
            (second_any, second_ref), (order_any, order_ref),
        ))
    ]
    small[0].start()
    load_frames(0).start()
    for copy in small[1:]:
        copy.start()
    for n in range(1, loads):
        load_frames(n).start()

    small[0].wait()
    for m in range(taps):
        tap = coef_in[pl.ds(m, width_a, stride=taps), :]
        for i in range(in_local):
            coef_ref[pl.ds(m * rows + i, width_a, stride=in_local), :] = tap
    for copy in small[1:]:
        copy.wait()

    def one_spectrum(t, carry):
        acc = None
        for m in range(taps):
            frame = x_ref[pl.ds(pl.multiple_of((t + m) * rows, rows), rows), :].astype(F32)
            term = coef_ref[m * rows:(m + 1) * rows, :] * frame
            acc = term if acc is None else acc + term
        out = jnp.dot(first_ref[...], acc.astype(BF16), preferred_element_type=F32)
        re, im = out[:rows], out[rows:]
        w_re, w_im = twist_ref[:rows, :], twist_ref[rows:, :]
        real_ref[pl.ds(t, rows, stride=slot), :] = re * w_re - im * w_im
        imag_ref[pl.ds(t, rows, stride=slot), :] = re * w_im + im * w_re
        return carry

    for n in range(loads):
        load_frames(n).wait()
        lax.fori_loop(n * t_load, (n + 1) * t_load, one_spectrum, 0, unroll=4)
    pl.semaphore_wait(barrier, peers - 1)

    per_dest = kept // peers * in_local

    def channel_pair(kp, carry):
        parts = []
        for kk in range(2):
            both = []
            for i in range(in_local):
                at = pl.ds(((kp * 2 + kk) * in_local + i) * slot, nspec)
                both.append(jnp.concatenate(
                    [real_ref[at, :].astype(BF16), imag_ref[at, :].astype(BF16)], axis=1
                ))
            both = jnp.concatenate(both, axis=0)
            res = lax.dot_general(second_ref[...], both, NT, preferred_element_type=F32)
            for i in range(in_local):
                cols = slice(i * nspec, (i + 1) * nspec)
                turn_ref[pl.ds(kk * kept * in_local + i, kept, stride=in_local), :] = (
                    jnp.concatenate([res[:kept, cols], res[kept:, cols]], axis=1)
                )
            part = turn_ref[kk * kept * in_local:(kk + 1) * kept * in_local, :]
            parts.append(part.reshape(peers, per_dest, 2 * nspec))
        send_ref[:, kp] = jnp.concatenate(parts, axis=1).astype(BF16)
        return carry

    def remote(c, o):
        dest = lax.rem(me + o, peers)
        at = pl.ds(c * step, step)
        return pltpu.make_async_remote_copy(
            src_ref=send_ref.at[dest, at], dst_ref=recv_ref.at[me, at],
            send_sem=send_sem.at[c, o], recv_sem=recv_sem.at[c, o],
            device_id={"inputs": dest}, device_id_type=pl.DeviceIdType.MESH,
        )

    def chunk(c, carry):
        lax.fori_loop(0, step, lambda n, u: channel_pair(c * step + n, u), 0, unroll=2)

        def push(n, carry):
            remote(c, lax.rem(n + peers // 2 - 1, peers - 1) + 1).start()
            return carry

        lax.fori_loop(0, peers - 1, push, 0)
        return carry

    lax.fori_loop(0, chunks, chunk, 0)
    own = pltpu.make_async_copy(send_ref.at[me], recv_ref.at[me], own_sem)
    own.start()
    own.wait()

    count = peers * in_local
    per = 2 * (kept // peers)
    halves = per // 2
    channels = pairs * per
    i_at = lax.broadcasted_iota(jnp.int32, (count, count), 0)
    j_at = lax.broadcasted_iota(jnp.int32, (count, count), 1)

    def correlate_pair(kp, carry):
        block_rows = recv_ref[:, kp].reshape(per * count, 2 * nspec)
        lined = jnp.dot(order_ref[...], block_rows, preferred_element_type=F32)
        turned = jnp.concatenate([-lined[:, nspec:], lined[:, :nspec]], axis=1).astype(BF16)
        lined = lined.astype(BF16)
        for s in range(per):
            block = lined[s * count:(s + 1) * count]
            rotated = turned[s * count:(s + 1) * count]
            re = lax.dot_general(block, block, NT, preferred_element_type=F32)
            im = lax.dot_general(block, rotated, NT, preferred_element_type=F32)
            vis = jnp.where(i_at >= j_at, re, im) * (1.0 / nspec)
            c = (s % halves) * 2 * pairs + kp * 2 + s // halves
            vis_ref[pl.ds(c, count // 2, stride=channels), :] = jnp.concatenate(
                [vis[:count // 2], vis[count // 2:]], axis=1
            )
        return carry

    def receive(c, carry):
        def arrive(o, carry):
            remote(c, o).wait_recv()
            return carry

        lax.fori_loop(1, peers, arrive, 0)
        lax.fori_loop(0, step, lambda n, u: correlate_pair(c * step + n, u), 0, unroll=2)
        return carry

    lax.fori_loop(0, chunks, receive, 0)

    def finish(n, carry):
        remote(n // (peers - 1), n % (peers - 1) + 1).wait_send()
        return carry

    lax.fori_loop(0, chunks * (peers - 1), finish, 0)


def turn_kernel(channels, vis_ref, out_ref):
    half = out_ref.shape[0] // 2
    width = out_ref.shape[1]

    def one_row(i, carry):
        block = vis_ref[pl.ds(pl.multiple_of(i * channels, channels), channels), :]
        block = block.T.astype(BF16)
        out_ref[i] = block[:width]
        out_ref[i + half] = block[width:]
        return carry

    lax.fori_loop(0, half, one_row, 0, unroll=4)


def kernel_body(peers, kept, samples, filter_coefs):
    in_local, total = samples.shape
    taps, nfft = filter_coefs.shape
    width_a = nfft // WIDTH_B
    nspec = total // nfft - taps + 1
    rows = width_a * in_local
    pairs = width_a // 2
    chunks = 8
    loads = 4
    pad = 1
    per = 2 * (kept // peers)
    count = peers * in_local
    channels = pairs * per
    x = samples.reshape(in_local, total // WIDTH_B, WIDTH_B).transpose(1, 0, 2)
    x = x.reshape(total // WIDTH_B * in_local, WIDTH_B)
    coefs = filter_coefs.reshape(taps, width_a, WIDTH_B).transpose(1, 0, 2)
    coefs = coefs.reshape(width_a * taps, WIDTH_B)
    first, twist, second = make_tables(in_local, width_a, kept)
    order = np.zeros((per, peers, in_local, peers, per, in_local), np.float32)
    for s in range(per):
        for p in range(peers):
            order[s, p, range(in_local), p, s, range(in_local)] = 1
    order = jnp.asarray(order.reshape(per * count, per * count), BF16)
    blocks = (peers, pairs, per * in_local, 2 * nspec)
    inputs = (x, coefs, first, twist, second, order)
    vis = pl.pallas_call(
        functools.partial(
            correlator_kernel, (peers, in_local, nspec, taps, kept, chunks, loads, pad)
        ),
        out_shape=jax.ShapeDtypeStruct((count // 2 * channels, 2 * count), F32),
        in_specs=[pl.BlockSpec(memory_space=pl.ANY)] * len(inputs),
        out_specs=pl.BlockSpec(memory_space=pltpu.VMEM),
        scratch_shapes=[pltpu.VMEM(a.shape, a.dtype) for a in inputs] + [
            pltpu.VMEM((taps * rows, WIDTH_B), F32),
            pltpu.VMEM((rows * (nspec + pad), WIDTH_B), F32),
            pltpu.VMEM((rows * (nspec + pad), WIDTH_B), F32),
            pltpu.VMEM((2 * kept * in_local, 2 * nspec), F32),
            pltpu.VMEM(blocks, BF16),
            pltpu.VMEM(blocks, BF16),
            pltpu.SemaphoreType.DMA((len(inputs) - 1,)),
            pltpu.SemaphoreType.DMA((loads,)),
            pltpu.SemaphoreType.DMA((chunks, peers)),
            pltpu.SemaphoreType.DMA((chunks, peers)),
            pltpu.SemaphoreType.DMA,
        ],
        compiler_params=pltpu.CompilerParams(
            collective_id=0, has_side_effects=True, vmem_limit_bytes=56 * 2**20
        ),
        name="correlator",
    )(*inputs)
    out = pl.pallas_call(
        functools.partial(turn_kernel, channels),
        out_shape=jax.ShapeDtypeStruct((count, count, channels), BF16),
        in_specs=[pl.BlockSpec(memory_space=pltpu.VMEM)],
        out_specs=pl.BlockSpec(memory_space=pltpu.VMEM),
        compiler_params=pltpu.CompilerParams(vmem_limit_bytes=32 * 2**20),
        name="turn",
    )(vis)
    return out.transpose(2, 0, 1)


def solution(mesh):
    peers = mesh.shape["inputs"]

    def body(samples, filter_coefs):
        in_local = samples.shape[0]
        kept = WIDTH_B // 4
        whole_q = kept % peers == 0
        if whole_q and (2 * in_local * (kept // peers)) % 16 == 0:
            return kernel_body(peers, kept, samples, filter_coefs)
        return plain_body(samples, filter_coefs)

    return jax.shard_map(
        body,
        mesh=mesh,
        in_specs=(P(("groups", "inputs"), None), P()),
        out_specs=P(("groups", "inputs"), None, None),
        check_vma=False,
    )
```

```python
import functools
import math

import jax
import jax.numpy as jnp
import numpy as np
from jax import lax
from jax.experimental import pallas as pl
from jax.experimental.pallas import tpu as pltpu
from jax.sharding import PartitionSpec as P


def phase_table(first, second, period):
    rows = lax.broadcasted_iota(jnp.int32, (first, second), 0)
    cols = lax.broadcasted_iota(jnp.int32, (first, second), 1)
    angle = 2.0 * math.pi / period * (rows * cols % period).astype(jnp.float32)
    return (jnp.cos(angle), -jnp.sin(angle))


def correlate_items(block):
    count = block.shape[0]
    nspec_local = block.shape[2] // 2
    rotated = jnp.concatenate([-block[..., nspec_local:], block[..., :nspec_local]], axis=-1)
    real_sum = jnp.einsum("ikt,jkt->kij", block, block, preferred_element_type=jnp.float32)
    imag_sum = jnp.einsum("ikt,jkt->kij", block, rotated, preferred_element_type=jnp.float32)
    rows = lax.broadcasted_iota(jnp.int32, (count, count), 0)
    cols = lax.broadcasted_iota(jnp.int32, (count, count), 1)
    return (jnp.where(rows >= cols, real_sum, imag_sum) / nspec_local).astype(jnp.bfloat16)


def correlate_turned(block):
    flat_block = block.reshape(block.shape[0], block.shape[2], block.shape[3])
    return correlate_items(flat_block)


def plain_body(samples, filter_coefs):
    in_local, total = samples.shape
    taps_count, nfft_local = filter_coefs.shape
    frame_count = total // nfft_local
    nspec_local = frame_count - taps_count + 1
    width_b = 128
    width_a = nfft_local // width_b
    kept_width = width_b // 4
    frames = samples.reshape(in_local, frame_count, nfft_local).astype(jnp.float32)
    filtered = filter_coefs[0] * frames[:, 0:nspec_local]
    for tap_index in range(1, taps_count):
        filtered = (
            filtered + filter_coefs[tap_index] * frames[:, tap_index : tap_index + nspec_local]
        )
    grid_view = filtered.astype(jnp.bfloat16).reshape(in_local, nspec_local, width_a, width_b)
    first_cos, first_sin = phase_table(width_a, width_a, width_a)
    first_table = jnp.concatenate([first_cos, first_sin], axis=1).astype(jnp.bfloat16)
    first_out = jnp.einsum(
        "itab,ak->itkb", grid_view, first_table, preferred_element_type=jnp.float32
    )
    real_one = first_out[:, :, :width_a]
    imag_one = first_out[:, :, width_a:]
    twist_cos, twist_sin = phase_table(width_a, width_b, nfft_local)
    real_two = real_one * twist_cos - imag_one * twist_sin
    imag_two = real_one * twist_sin + imag_one * twist_cos
    stacked = jnp.concatenate(
        [real_two.astype(jnp.bfloat16), imag_two.astype(jnp.bfloat16)], axis=3
    )
    second_cos, second_sin = phase_table(width_b, width_b, width_b)
    second_cos = second_cos[:, :kept_width]
    second_sin = second_sin[:, :kept_width]
    upper_rows = jnp.concatenate([second_cos, second_sin], axis=1)
    lower_rows = jnp.concatenate([-second_sin, second_cos], axis=1)
    second_table = jnp.concatenate([upper_rows, lower_rows], axis=0).astype(jnp.bfloat16)
    second_out = jnp.einsum(
        "itkn,nq->iqkt", stacked, second_table, preferred_element_type=jnp.float32
    )
    real_out = second_out[:, :kept_width]
    imag_out = second_out[:, kept_width:]
    channels = width_a * kept_width
    spectra = jnp.concatenate(
        [real_out.astype(jnp.bfloat16), imag_out.astype(jnp.bfloat16)], axis=3
    )
    spectra = spectra.reshape(in_local, channels, 2 * nspec_local)
    peers = lax.axis_size("inputs")
    per_peer = channels // peers
    owner_view = spectra.reshape(in_local, peers, per_peer, 2 * nspec_local)
    result = correlate_turned(
        lax.all_to_all(owner_view, "inputs", split_axis=1, concat_axis=0, tiled=True)
    )
    return result


WIDTH_B = 128
BF16 = jnp.bfloat16
F32 = jnp.float32
NT = (((1,), (1,)), ((), ()))


def np_phase(first, second, period):
    turns = np.outer(np.arange(first), np.arange(second)) % period
    angle = np.float32(2.0 * math.pi / period) * turns.astype(np.float32)
    return np.cos(angle), -np.sin(angle)


def make_tables(in_local, width_a, kept):
    nfft = width_a * WIDTH_B
    first = np.concatenate([t.T for t in np_phase(width_a, width_a, width_a)], axis=0)
    first = np.kron(first, np.eye(in_local, dtype=np.float32))
    twist = np.concatenate(
        [np.repeat(t, in_local, axis=0) for t in np_phase(width_a, WIDTH_B, nfft)], axis=0
    )
    cos_b, sin_b = (t[:, :kept].T for t in np_phase(WIDTH_B, WIDTH_B, WIDTH_B))
    second = np.concatenate(
        [np.concatenate([cos_b, -sin_b], axis=1), np.concatenate([sin_b, cos_b], axis=1)], axis=0
    )
    return jnp.asarray(first, BF16), jnp.asarray(twist, F32), jnp.asarray(second, BF16)


def correlator_kernel(
    dims, x_any, coef_any, first_any, twist_any, second_any, order_any, half_ref,
    x_ref, coef_in, first_ref, twist_ref, second_ref, order_ref, coef_ref,
    real_ref, imag_ref, turn_ref, send_ref, recv_ref, vis_ref,
    load_sem, x_sem, send_sem, recv_sem, own_sem,
):
    peers, in_local, nspec, taps, kept, chunks, loads, pad = dims
    rows = first_ref.shape[1]
    width_a = rows // in_local
    pairs = width_a // 2
    step = pairs // chunks
    slot = nspec + pad
    me = lax.axis_index("inputs")

    barrier = pltpu.get_barrier_semaphore()

    def greet(o, carry):
        pl.semaphore_signal(
            barrier, inc=1, device_id={"inputs": lax.rem(me + o, peers)},
            device_id_type=pl.DeviceIdType.MESH,
        )
        return carry

    lax.fori_loop(1, peers, greet, 0)

    t_load = nspec // loads

    def load_frames(n):
        start = 0 if n == 0 else n * t_load + taps - 1
        at = pl.ds(start * rows, ((n + 1) * t_load + taps - 1 - start) * rows)
        return pltpu.make_async_copy(x_any.at[at], x_ref.at[at], x_sem.at[n])

    small = [
        pltpu.make_async_copy(src, dst, load_sem.at[n])
        for n, (src, dst) in enumerate((
            (coef_any, coef_in), (first_any, first_ref), (twist_any, twist_ref),
            (second_any, second_ref), (order_any, order_ref),
        ))
    ]
    small[0].start()
    load_frames(0).start()
    for copy in small[1:]:
        copy.start()
    for n in range(1, loads):
        load_frames(n).start()

    small[0].wait()
    for m in range(taps):
        tap = coef_in[pl.ds(m, width_a, stride=taps), :]
        for i in range(in_local):
            coef_ref[pl.ds(m * rows + i, width_a, stride=in_local), :] = tap
    for copy in small[1:]:
        copy.wait()

    lane_block = 64

    def two_spectra(tp, carry):
        t = tp * 2
        filtered = []
        for r in range(0, rows, lane_block):
            frames = [
                x_ref[pl.ds(pl.multiple_of((t + m) * rows + r, lane_block), lane_block), :].astype(F32)
                for m in range(taps + 1)
            ]
            pair = []
            for late in range(2):
                acc = None
                for m in range(taps):
                    at = m * rows + r
                    term = coef_ref[at:at + lane_block, :] * frames[m + late]
                    acc = term if acc is None else acc + term
                pair.append(acc.astype(BF16))
            filtered.append(jnp.concatenate(pair, axis=1))
        filtered = jnp.concatenate(filtered, axis=0)
        out = jnp.dot(first_ref[...], filtered, preferred_element_type=F32)
        w_re, w_im = twist_ref[:rows, :], twist_ref[rows:, :]
        for late in range(2):
            cols = slice(late * WIDTH_B, (late + 1) * WIDTH_B)
            re, im = out[:rows, cols], out[rows:, cols]
            real_ref[pl.ds(t + late, rows, stride=slot), :] = re * w_re - im * w_im
            imag_ref[pl.ds(t + late, rows, stride=slot), :] = re * w_im + im * w_re
        return carry

    for n in range(loads):
        load_frames(n).wait()
        lax.fori_loop(n * t_load // 2, (n + 1) * t_load // 2, two_spectra, 0, unroll=4)
    pl.semaphore_wait(barrier, peers - 1)

    per_dest = kept // peers * in_local

    def channel_pair(kp, carry):
        parts = []
        for kk in range(2):
            both = []
            for i in range(in_local):
                at = pl.ds(((kp * 2 + kk) * in_local + i) * slot, nspec)
                both.append(jnp.concatenate(
                    [real_ref[at, :].astype(BF16), imag_ref[at, :].astype(BF16)], axis=1
                ))
            both = jnp.concatenate(both, axis=0)
            res = lax.dot_general(second_ref[...], both, NT, preferred_element_type=F32)
            for i in range(in_local):
                cols = slice(i * nspec, (i + 1) * nspec)
                turn_ref[pl.ds(kk * kept * in_local + i, kept, stride=in_local), :] = (
                    jnp.concatenate([res[:kept, cols], res[kept:, cols]], axis=1)
                )
            part = turn_ref[kk * kept * in_local:(kk + 1) * kept * in_local, :]
            parts.append(part.reshape(peers, per_dest, 2 * nspec))
        send_ref[:, kp] = jnp.concatenate(parts, axis=1).astype(BF16)
        return carry

    def remote(c, o):
        dest = lax.rem(me + o, peers)
        at = pl.ds(c * step, step)
        return pltpu.make_async_remote_copy(
            src_ref=send_ref.at[dest, at], dst_ref=recv_ref.at[me, at],
            send_sem=send_sem.at[c, o], recv_sem=recv_sem.at[c, o],
            device_id={"inputs": dest}, device_id_type=pl.DeviceIdType.MESH,
        )

    def chunk(c, carry):
        lax.fori_loop(0, step, lambda n, u: channel_pair(c * step + n, u), 0, unroll=2)

        def push(n, carry):
            remote(c, lax.rem(n + peers // 2 - 1, peers - 1) + 1).start()
            return carry

        lax.fori_loop(0, peers - 1, push, 0)
        return carry

    lax.fori_loop(0, chunks, chunk, 0)
    own = pltpu.make_async_copy(send_ref.at[me], recv_ref.at[me], own_sem)
    own.start()
    own.wait()

    count = peers * in_local
    per = 2 * (kept // peers)
    halves = per // 2
    channels = pairs * per
    i_at = lax.broadcasted_iota(jnp.int32, (count, count), 0)
    j_at = lax.broadcasted_iota(jnp.int32, (count, count), 1)

    def correlate_pair(kp, carry):
        block_rows = recv_ref[:, kp].reshape(per * count, 2 * nspec)
        lined = jnp.dot(order_ref[...], block_rows, preferred_element_type=F32)
        turned = jnp.concatenate([-lined[:, nspec:], lined[:, :nspec]], axis=1).astype(BF16)
        lined = lined.astype(BF16)
        for s in range(per):
            block = lined[s * count:(s + 1) * count]
            rotated = turned[s * count:(s + 1) * count]
            re = lax.dot_general(block, block, NT, preferred_element_type=F32)
            im = lax.dot_general(block, rotated, NT, preferred_element_type=F32)
            vis = jnp.where(i_at >= j_at, re, im) * (1.0 / nspec)
            c = (s % halves) * 2 * pairs + kp * 2 + s // halves
            vis_ref[pl.ds(c, count // 2, stride=channels), :] = jnp.concatenate(
                [vis[:count // 2], vis[count // 2:]], axis=1
            )
        return carry

    def receive(c, carry):
        def arrive(o, carry):
            remote(c, o).wait_recv()
            return carry

        lax.fori_loop(1, peers, arrive, 0)
        lax.fori_loop(0, step, lambda n, u: correlate_pair(c * step + n, u), 0, unroll=2)
        return carry

    lax.fori_loop(0, chunks, receive, 0)
    half_ref[...] = vis_ref[...].astype(BF16)

    def finish(n, carry):
        remote(n // (peers - 1), n % (peers - 1) + 1).wait_send()
        return carry

    lax.fori_loop(0, chunks * (peers - 1), finish, 0)


def turn_kernel(channels, vis_ref, out_ref):
    half = out_ref.shape[0] // 2
    width = out_ref.shape[1]

    def one_row(i, carry):
        block = vis_ref[pl.ds(pl.multiple_of(i * channels, channels), channels), :]
        block = block.astype(F32).T.astype(BF16)
        out_ref[i] = block[:width]
        out_ref[i + half] = block[width:]
        return carry

    lax.fori_loop(0, half, one_row, 0, unroll=4)


def kernel_body(peers, kept, samples, filter_coefs):
    in_local, total = samples.shape
    taps, nfft = filter_coefs.shape
    width_a = nfft // WIDTH_B
    nspec = total // nfft - taps + 1
    rows = width_a * in_local
    pairs = width_a // 2
    chunks = 8
    loads = 4
    pad = 1
    per = 2 * (kept // peers)
    count = peers * in_local
    channels = pairs * per
    x = samples.reshape(in_local, total // WIDTH_B, WIDTH_B).transpose(1, 0, 2)
    x = x.reshape(total // WIDTH_B * in_local, WIDTH_B)
    coefs = filter_coefs.reshape(taps, width_a, WIDTH_B).transpose(1, 0, 2)
    coefs = coefs.reshape(width_a * taps, WIDTH_B)
    first, twist, second = make_tables(in_local, width_a, kept)
    order = np.zeros((per, peers, in_local, peers, per, in_local), np.float32)
    for s in range(per):
        for p in range(peers):
            order[s, p, range(in_local), p, s, range(in_local)] = 1
    order = jnp.asarray(order.reshape(per * count, per * count), BF16)
    blocks = (peers, pairs, per * in_local, 2 * nspec)
    inputs = (x, coefs, first, twist, second, order)
    vis = pl.pallas_call(
        functools.partial(
            correlator_kernel, (peers, in_local, nspec, taps, kept, chunks, loads, pad)
        ),
        out_shape=jax.ShapeDtypeStruct((count // 2 * channels, 2 * count), BF16),
        in_specs=[pl.BlockSpec(memory_space=pl.ANY)] * len(inputs),
        out_specs=pl.BlockSpec(memory_space=pltpu.VMEM),
        scratch_shapes=[pltpu.VMEM(a.shape, a.dtype) for a in inputs] + [
            pltpu.VMEM((taps * rows, WIDTH_B), F32),
            pltpu.VMEM((rows * (nspec + pad), WIDTH_B), F32),
            pltpu.VMEM((rows * (nspec + pad), WIDTH_B), F32),
            pltpu.VMEM((2 * kept * in_local, 2 * nspec), F32),
            pltpu.VMEM(blocks, BF16),
            pltpu.VMEM(blocks, BF16),
            pltpu.VMEM((count // 2 * channels, 2 * count), F32),
            pltpu.SemaphoreType.DMA((len(inputs) - 1,)),
            pltpu.SemaphoreType.DMA((loads,)),
            pltpu.SemaphoreType.DMA((chunks, peers)),
            pltpu.SemaphoreType.DMA((chunks, peers)),
            pltpu.SemaphoreType.DMA,
        ],
        compiler_params=pltpu.CompilerParams(
            collective_id=0, has_side_effects=True, vmem_limit_bytes=56 * 2**20
        ),
        name="correlator",
    )(*inputs)
    out = pl.pallas_call(
        functools.partial(turn_kernel, channels),
        out_shape=jax.ShapeDtypeStruct((count, count, channels), BF16),
        in_specs=[pl.BlockSpec(memory_space=pltpu.VMEM)],
        out_specs=pl.BlockSpec(memory_space=pltpu.VMEM),
        compiler_params=pltpu.CompilerParams(vmem_limit_bytes=32 * 2**20),
        name="turn",
    )(vis)
    return out.transpose(2, 0, 1)


def solution(mesh):
    peers = mesh.shape["inputs"]

    def body(samples, filter_coefs):
        in_local = samples.shape[0]
        kept = WIDTH_B // 4
        whole_q = kept % peers == 0
        if whole_q and (2 * in_local * (kept // peers)) % 16 == 0:
            return kernel_body(peers, kept, samples, filter_coefs)
        return plain_body(samples, filter_coefs)

    return jax.shard_map(
        body,
        mesh=mesh,
        in_specs=(P(("groups", "inputs"), None), P()),
        out_specs=P(("groups", "inputs"), None, None),
        check_vma=False,
    )
```

```python
import functools
import math

import jax
import jax.numpy as jnp
import numpy as np
from jax import lax
from jax.experimental import pallas as pl
from jax.experimental.pallas import tpu as pltpu
from jax.sharding import PartitionSpec as P


def phase_table(first, second, period):
    rows = lax.broadcasted_iota(jnp.int32, (first, second), 0)
    cols = lax.broadcasted_iota(jnp.int32, (first, second), 1)
    angle = 2.0 * math.pi / period * (rows * cols % period).astype(jnp.float32)
    return (jnp.cos(angle), -jnp.sin(angle))


def correlate_items(block):
    count = block.shape[0]
    nspec_local = block.shape[2] // 2
    rotated = jnp.concatenate([-block[..., nspec_local:], block[..., :nspec_local]], axis=-1)
    real_sum = jnp.einsum("ikt,jkt->kij", block, block, preferred_element_type=jnp.float32)
    imag_sum = jnp.einsum("ikt,jkt->kij", block, rotated, preferred_element_type=jnp.float32)
    rows = lax.broadcasted_iota(jnp.int32, (count, count), 0)
    cols = lax.broadcasted_iota(jnp.int32, (count, count), 1)
    return (jnp.where(rows >= cols, real_sum, imag_sum) / nspec_local).astype(jnp.bfloat16)


def correlate_turned(block):
    flat_block = block.reshape(block.shape[0], block.shape[2], block.shape[3])
    return correlate_items(flat_block)


def plain_body(samples, filter_coefs):
    in_local, total = samples.shape
    taps_count, nfft_local = filter_coefs.shape
    frame_count = total // nfft_local
    nspec_local = frame_count - taps_count + 1
    width_b = 128
    width_a = nfft_local // width_b
    kept_width = width_b // 4
    frames = samples.reshape(in_local, frame_count, nfft_local).astype(jnp.float32)
    filtered = filter_coefs[0] * frames[:, 0:nspec_local]
    for tap_index in range(1, taps_count):
        filtered = (
            filtered + filter_coefs[tap_index] * frames[:, tap_index : tap_index + nspec_local]
        )
    grid_view = filtered.astype(jnp.bfloat16).reshape(in_local, nspec_local, width_a, width_b)
    first_cos, first_sin = phase_table(width_a, width_a, width_a)
    first_table = jnp.concatenate([first_cos, first_sin], axis=1).astype(jnp.bfloat16)
    first_out = jnp.einsum(
        "itab,ak->itkb", grid_view, first_table, preferred_element_type=jnp.float32
    )
    real_one = first_out[:, :, :width_a]
    imag_one = first_out[:, :, width_a:]
    twist_cos, twist_sin = phase_table(width_a, width_b, nfft_local)
    real_two = real_one * twist_cos - imag_one * twist_sin
    imag_two = real_one * twist_sin + imag_one * twist_cos
    stacked = jnp.concatenate(
        [real_two.astype(jnp.bfloat16), imag_two.astype(jnp.bfloat16)], axis=3
    )
    second_cos, second_sin = phase_table(width_b, width_b, width_b)
    second_cos = second_cos[:, :kept_width]
    second_sin = second_sin[:, :kept_width]
    upper_rows = jnp.concatenate([second_cos, second_sin], axis=1)
    lower_rows = jnp.concatenate([-second_sin, second_cos], axis=1)
    second_table = jnp.concatenate([upper_rows, lower_rows], axis=0).astype(jnp.bfloat16)
    second_out = jnp.einsum(
        "itkn,nq->iqkt", stacked, second_table, preferred_element_type=jnp.float32
    )
    real_out = second_out[:, :kept_width]
    imag_out = second_out[:, kept_width:]
    channels = width_a * kept_width
    spectra = jnp.concatenate(
        [real_out.astype(jnp.bfloat16), imag_out.astype(jnp.bfloat16)], axis=3
    )
    spectra = spectra.reshape(in_local, channels, 2 * nspec_local)
    peers = lax.axis_size("inputs")
    per_peer = channels // peers
    owner_view = spectra.reshape(in_local, peers, per_peer, 2 * nspec_local)
    result = correlate_turned(
        lax.all_to_all(owner_view, "inputs", split_axis=1, concat_axis=0, tiled=True)
    )
    return result


WIDTH_B = 128
BF16 = jnp.bfloat16
F32 = jnp.float32
NT = (((1,), (1,)), ((), ()))


def np_phase(first, second, period):
    turns = np.outer(np.arange(first), np.arange(second)) % period
    angle = np.float32(2.0 * math.pi / period) * turns.astype(np.float32)
    return np.cos(angle), -np.sin(angle)


def make_tables(in_local, width_a, kept):
    nfft = width_a * WIDTH_B
    first = np.concatenate([t.T for t in np_phase(width_a, width_a, width_a)], axis=0)
    first = np.kron(first, np.eye(in_local, dtype=np.float32))
    twist = np.concatenate(
        [np.repeat(t, in_local, axis=0) for t in np_phase(width_a, WIDTH_B, nfft)], axis=0
    )
    cos_b, sin_b = (t[:, :kept].T for t in np_phase(WIDTH_B, WIDTH_B, WIDTH_B))
    second = np.concatenate(
        [np.concatenate([cos_b, -sin_b], axis=1), np.concatenate([sin_b, cos_b], axis=1)], axis=0
    )
    return jnp.asarray(first, BF16), jnp.asarray(twist, F32), jnp.asarray(second, BF16)


def correlator_kernel(
    dims, x_any, coef_any, first_any, twist_any, second_any, order_any, half_ref,
    x_ref, coef_in, first_ref, twist_ref, second_ref, order_ref, coef_ref,
    real_ref, imag_ref, turn_ref, send_ref, recv_ref, vis_ref,
    load_sem, x_sem, send_sem, recv_sem, own_sem,
):
    peers, in_local, nspec, taps, kept, chunks, loads, pad = dims
    rows = first_ref.shape[1]
    width_a = rows // in_local
    pairs = width_a // 2
    step = pairs // chunks
    slot = nspec + pad
    me = lax.axis_index("inputs")

    barrier = pltpu.get_barrier_semaphore()

    def greet(o, carry):
        pl.semaphore_signal(
            barrier, inc=1, device_id={"inputs": lax.rem(me + o, peers)},
            device_id_type=pl.DeviceIdType.MESH,
        )
        return carry

    lax.fori_loop(1, peers, greet, 0)

    t_load = nspec // loads

    def load_frames(n):
        start = 0 if n == 0 else n * t_load + taps - 1
        at = pl.ds(start * rows, ((n + 1) * t_load + taps - 1 - start) * rows)
        return pltpu.make_async_copy(x_any.at[at], x_ref.at[at], x_sem.at[n])

    small = [
        pltpu.make_async_copy(src, dst, load_sem.at[n])
        for n, (src, dst) in enumerate((
            (coef_any, coef_in), (first_any, first_ref), (twist_any, twist_ref),
            (second_any, second_ref), (order_any, order_ref),
        ))
    ]
    small[0].start()
    load_frames(0).start()
    for copy in small[1:]:
        copy.start()
    for n in range(1, loads):
        load_frames(n).start()

    small[0].wait()
    for m in range(taps):
        tap = coef_in[pl.ds(m, width_a, stride=taps), :]
        for i in range(in_local):
            coef_ref[pl.ds(m * rows + i, width_a, stride=in_local), :] = tap
    for copy in small[1:]:
        copy.wait()

    lane_block = 64

    def two_spectra(tp, carry):
        t = tp * 2
        filtered = []
        for r in range(0, rows, lane_block):
            frames = [
                x_ref[pl.ds(pl.multiple_of((t + m) * rows + r, lane_block), lane_block), :].astype(F32)
                for m in range(taps + 1)
            ]
            pair = []
            for late in range(2):
                acc = None
                for m in range(taps):
                    at = m * rows + r
                    term = coef_ref[at:at + lane_block, :] * frames[m + late]
                    acc = term if acc is None else acc + term
                pair.append(acc.astype(BF16))
            filtered.append(jnp.concatenate(pair, axis=1))
        filtered = jnp.concatenate(filtered, axis=0)
        out = jnp.dot(first_ref[...], filtered, preferred_element_type=F32)
        w_re, w_im = twist_ref[:rows, :], twist_ref[rows:, :]
        for late in range(2):
            cols = slice(late * WIDTH_B, (late + 1) * WIDTH_B)
            re, im = out[:rows, cols], out[rows:, cols]
            real_ref[pl.ds(t + late, rows, stride=slot), :] = re * w_re - im * w_im
            imag_ref[pl.ds(t + late, rows, stride=slot), :] = re * w_im + im * w_re
        return carry

    for n in range(loads):
        load_frames(n).wait()
        lax.fori_loop(n * t_load // 2, (n + 1) * t_load // 2, two_spectra, 0, unroll=4)
    pl.semaphore_wait(barrier, peers - 1)

    per_dest = kept // peers * in_local

    def channel_pair(kp, carry):
        parts = []
        for kk in range(2):
            both = []
            for i in range(in_local):
                at = pl.ds(((kp * 2 + kk) * in_local + i) * slot, nspec)
                both.append(jnp.concatenate(
                    [real_ref[at, :].astype(BF16), imag_ref[at, :].astype(BF16)], axis=1
                ))
            both = jnp.concatenate(both, axis=0)
            res = lax.dot_general(second_ref[...], both, NT, preferred_element_type=F32)
            for i in range(in_local):
                cols = slice(i * nspec, (i + 1) * nspec)
                turn_ref[pl.ds(kk * kept * in_local + i, kept, stride=in_local), :] = (
                    jnp.concatenate([res[:kept, cols], res[kept:, cols]], axis=1)
                )
            part = turn_ref[kk * kept * in_local:(kk + 1) * kept * in_local, :]
            parts.append(part.reshape(peers, per_dest, 2 * nspec))
        send_ref[:, kp] = jnp.concatenate(parts, axis=1).astype(BF16)
        return carry

    def remote(c, o):
        dest = lax.rem(me + o, peers)
        at = pl.ds(c * step, step)
        return pltpu.make_async_remote_copy(
            src_ref=send_ref.at[dest, at], dst_ref=recv_ref.at[me, at],
            send_sem=send_sem.at[c, o], recv_sem=recv_sem.at[c, o],
            device_id={"inputs": dest}, device_id_type=pl.DeviceIdType.MESH,
        )

    def chunk(c, carry):
        lax.fori_loop(0, step, lambda n, u: channel_pair(c * step + n, u), 0, unroll=2)

        def push(n, carry):
            remote(c, lax.rem(n + peers // 2 - 1, peers - 1) + 1).start()
            return carry

        lax.fori_loop(0, peers - 1, push, 0)
        return carry

    lax.fori_loop(0, chunks, chunk, 0)
    own = pltpu.make_async_copy(send_ref.at[me], recv_ref.at[me], own_sem)
    own.start()
    own.wait()

    count = peers * in_local
    per = 2 * (kept // peers)
    halves = per // 2
    channels = pairs * per
    i_at = lax.broadcasted_iota(jnp.int32, (count, count), 0)
    j_at = lax.broadcasted_iota(jnp.int32, (count, count), 1)

    def correlate_pair(kp, carry):
        block_rows = recv_ref[:, kp].reshape(per * count, 2 * nspec)
        lined = jnp.dot(order_ref[...], block_rows, preferred_element_type=F32)
        turned = jnp.concatenate([-lined[:, nspec:], lined[:, :nspec]], axis=1).astype(BF16)
        lined = lined.astype(BF16)
        for s in range(per):
            block = lined[s * count:(s + 1) * count]
            rotated = turned[s * count:(s + 1) * count]
            re = lax.dot_general(block, block, NT, preferred_element_type=F32)
            im = lax.dot_general(block, rotated, NT, preferred_element_type=F32)
            vis = jnp.where(i_at >= j_at, re, im) * (1.0 / nspec)
            c = (s % halves) * 2 * pairs + kp * 2 + s // halves
            vis_ref[pl.ds(c, count // 2, stride=channels), :] = jnp.concatenate(
                [vis[:count // 2], vis[count // 2:]], axis=1
            )
        return carry

    def receive(c, carry):
        def arrive(o, carry):
            remote(c, o).wait()
            return carry

        lax.fori_loop(1, peers, arrive, 0)
        lax.fori_loop(0, step, lambda n, u: correlate_pair(c * step + n, u), 0, unroll=2)
        return carry

    lax.fori_loop(0, chunks, receive, 0)
    half_ref[...] = vis_ref[...].astype(BF16)


def turn_kernel(channels, vis_ref, out_ref):
    half = out_ref.shape[0] // 2
    width = out_ref.shape[1]

    def one_row(i, carry):
        block = vis_ref[pl.ds(pl.multiple_of(i * channels, channels), channels), :]
        block = block.astype(F32).T.astype(BF16)
        out_ref[i] = block[:width]
        out_ref[i + half] = block[width:]
        return carry

    lax.fori_loop(0, half, one_row, 0, unroll=4)


def kernel_body(peers, kept, samples, filter_coefs):
    in_local, total = samples.shape
    taps, nfft = filter_coefs.shape
    width_a = nfft // WIDTH_B
    nspec = total // nfft - taps + 1
    rows = width_a * in_local
    pairs = width_a // 2
    chunks = 8
    loads = 4
    pad = 1
    per = 2 * (kept // peers)
    count = peers * in_local
    channels = pairs * per
    x = samples.reshape(in_local, total // WIDTH_B, WIDTH_B).transpose(1, 0, 2)
    x = x.reshape(total // WIDTH_B * in_local, WIDTH_B)
    coefs = filter_coefs.reshape(taps, width_a, WIDTH_B).transpose(1, 0, 2)
    coefs = coefs.reshape(width_a * taps, WIDTH_B)
    first, twist, second = make_tables(in_local, width_a, kept)
    order = np.zeros((per, peers, in_local, peers, per, in_local), np.float32)
    for s in range(per):
        for p in range(peers):
            order[s, p, range(in_local), p, s, range(in_local)] = 1
    order = jnp.asarray(order.reshape(per * count, per * count), BF16)
    blocks = (peers, pairs, per * in_local, 2 * nspec)
    inputs = (x, coefs, first, twist, second, order)
    vis = pl.pallas_call(
        functools.partial(
            correlator_kernel, (peers, in_local, nspec, taps, kept, chunks, loads, pad)
        ),
        out_shape=jax.ShapeDtypeStruct((count // 2 * channels, 2 * count), BF16),
        in_specs=[pl.BlockSpec(memory_space=pl.ANY)] * len(inputs),
        out_specs=pl.BlockSpec(memory_space=pltpu.VMEM),
        scratch_shapes=[pltpu.VMEM(a.shape, a.dtype) for a in inputs] + [
            pltpu.VMEM((taps * rows, WIDTH_B), F32),
            pltpu.VMEM((rows * (nspec + pad), WIDTH_B), F32),
            pltpu.VMEM((rows * (nspec + pad), WIDTH_B), F32),
            pltpu.VMEM((2 * kept * in_local, 2 * nspec), F32),
            pltpu.VMEM(blocks, BF16),
            pltpu.VMEM(blocks, BF16),
            pltpu.VMEM((count // 2 * channels, 2 * count), F32),
            pltpu.SemaphoreType.DMA((len(inputs) - 1,)),
            pltpu.SemaphoreType.DMA((loads,)),
            pltpu.SemaphoreType.DMA((chunks, peers)),
            pltpu.SemaphoreType.DMA((chunks, peers)),
            pltpu.SemaphoreType.DMA,
        ],
        compiler_params=pltpu.CompilerParams(
            collective_id=0, has_side_effects=True, vmem_limit_bytes=56 * 2**20
        ),
        name="correlator",
    )(*inputs)
    out = pl.pallas_call(
        functools.partial(turn_kernel, channels),
        out_shape=jax.ShapeDtypeStruct((count, count, channels), BF16),
        in_specs=[pl.BlockSpec(memory_space=pltpu.VMEM)],
        out_specs=pl.BlockSpec(memory_space=pltpu.VMEM),
        compiler_params=pltpu.CompilerParams(vmem_limit_bytes=32 * 2**20),
        name="turn",
    )(vis)
    return out.transpose(2, 0, 1)


def solution(mesh):
    peers = mesh.shape["inputs"]

    def body(samples, filter_coefs):
        in_local = samples.shape[0]
        kept = WIDTH_B // 4
        whole_q = kept % peers == 0
        if whole_q and (2 * in_local * (kept // peers)) % 16 == 0:
            return kernel_body(peers, kept, samples, filter_coefs)
        return plain_body(samples, filter_coefs)

    return jax.shard_map(
        body,
        mesh=mesh,
        in_specs=(P(("groups", "inputs"), None), P()),
        out_specs=P(("groups", "inputs"), None, None),
        check_vma=False,
    )
```
